128 devices in a mesh: inst: 8 (over z, x_lo), tp: 16 (over x_hi, y, core).
Axes of the slice: x: 4 (x_hi: 2, x_lo: 2; x = x_hi * 2 + x_lo), y: 4, z: 4, core: 2. Of those that a mesh axis runs over, the one named last changes fastest.
Arguments:
- x_steps: bfloat16 [2, 512, 8192], P(None, 'inst', 'tp'), may hold values from -6 to 6
- norm_gain: float32 [8192], replicated, may hold values from 0.1 to 1.9
- w_query: bfloat16 [8192, 8192], P(None, 'tp'), may hold values from -0.0625 to 0.0625
- w_keyval: bfloat16 [8192, 2048], P(None, 'tp'), may hold values from -0.0625 to 0.0625
- w_out: bfloat16 [8192, 8192], P('tp'), may hold values from -0.375 to 0.375
- key_cache: bfloat16 [512, 16, 128, 256], P('inst', 'tp')
- lengths: int32 [512], replicated, may hold values from 1 to 256, as said below
- moved_slots: int32 [8, 8], replicated, may hold values from 0 to 63, as said below
- partner_mask: int32 [8], replicated, may hold values from 1 to 7
Outputs:
- attention_out: bfloat16 [2, 512, 8192], P(None, 'inst', 'tp')
- arrived: bfloat16 [64, 16, 128, 256], P('inst', 'tp')
The draws below stay inside these ranges and needn't reach their ends.
Inputs may be any that keep to these rules, and one draw needn't show every extreme that they name: `lengths`: some request has 256 cached tokens and some has 1. `moved_slots`: the 8 slots of one instance are distinct.
All inputs are finite; a program needn't handle non-finite values.
Results may differ from the reference program's by a relative error of at most 0.012.
The reference program's roundings to bfloat16 on the way count: a program that leaves them out, or rounds other values in their place, can miss the bound.
Values may be sent and summed in bfloat16 or wider, within the bound.
No kernel may reach another device: no remote copies, remote signals or barrier semaphores. Data moves between devices by JAX's collectives and lax.ppermute only.
A program may use at most 128 MiB of HBM per device.

```python
import math
from functools import reduce
import jax
import jax.numpy as jnp
from jax import lax

D = 8192
HEADS = 64
KVH = 8
HD = 128
REQ = 64
MOVE = 8
BLK = 128
GROUP = 2
INSTANCES = 8
N_TP = 16


def draw_key_cache(key, part):
    key = jax.random.fold_in(key, 11)
    key_one = jax.random.fold_in(key, 0)
    shape = (INSTANCES * REQ, N_TP, BLK, 2 * HD)
    values = jax.random.normal(key_one, shape, jnp.float32)
    return values.astype(jnp.bfloat16)


def draw_lengths(key, part):
    key = jax.random.fold_in(key, 5)
    key_one, key_two, key_three = jax.random.split(key, 3)
    total_rows = INSTANCES * REQ
    values = jax.random.randint(key_one, (total_rows,), 1, GROUP * BLK + 1)
    top_index = jax.random.randint(key_two, (), 0, total_rows)
    low_index = (top_index + 1 + jax.random.randint(key_three, (), 0, total_rows - 1)) % total_rows
    values = values.at[low_index].set(1).at[top_index].set(GROUP * BLK)
    return values.astype(jnp.int32)


def draw_moved_slots(key, part):
    key = jax.random.fold_in(key, 7)
    key_rows, key_extra = jax.random.split(key)
    row_keys = jax.random.split(key_rows, INSTANCES)
    slot_rows = jax.vmap(lambda row_key: jax.random.permutation(row_key, REQ)[:MOVE])(row_keys)
    inner = 1 + jax.random.permutation(key_extra, REQ - 2)[:MOVE - 2]
    first_row = jnp.concatenate([jnp.array([REQ - 1, 0], jnp.int32), inner.astype(jnp.int32)])
    slot_rows = slot_rows.astype(jnp.int32).at[0].set(first_row)
    return slot_rows


def place_ends(result, key, smallest, top_value):
    spot = [jax.random.randint(jax.random.fold_in(key, axis), (), 0, length) for axis, length in enumerate(result.shape)]
    widest = result.shape.index(max(result.shape))
    neighbour = spot[:widest] + [(spot[widest] + 1) % result.shape[widest]] + spot[widest + 1:]
    return result.at[tuple(spot)].set(smallest).at[tuple(neighbour)].set(top_value)


def block_levels(own_key, shape, cuts, smallest, largest):
    level, own = 1.0, jax.random.fold_in(own_key, 6)
    for dim, blocks in cuts:
        draws = jnp.exp(jax.random.uniform(jax.random.fold_in(own, dim), (blocks,), jnp.float32, smallest / len(cuts), largest / len(cuts)))
        level = level * jnp.repeat(draws, shape[dim] // blocks).reshape([-1 if axis == dim else 1 for axis in range(len(shape))])
    return level


def centred(stream_key, extent, scale, bound, shards=(), kind=jnp.bfloat16):
    drawn = scale * jax.random.normal(stream_key, extent, jnp.float32)
    if shards:
        drawn = drawn * block_levels(stream_key, extent, shards, -0.22, 0.18)
    return jnp.clip(drawn, -bound, bound).astype(kind)


def setup_inputs(seed: int = 0) -> dict:
    streams_of = jax.random.split(jax.random.key(seed), 10)
    x_steps = centred(streams_of[0], (2, INSTANCES * REQ, D), 1.0, 6.0, ((1, 8), (2, 16)))
    norm_gain = jnp.clip(1.0 + 0.18 * jax.random.normal(streams_of[1], (D,), jnp.float32), 0.1, 1.9)
    w_query = centred(streams_of[2], (D, HEADS * HD), D ** -0.5, 0.0625, ((1, 16),))
    w_keyval = centred(streams_of[3], (D, 2 * KVH * HD), D ** -0.5, 0.0625, ((1, 16),))
    w_out = centred(streams_of[4], (HEADS * HD, D), (D // 32) ** -0.5, 0.375, ((0, 16),))
    key_cache = draw_key_cache(jax.random.fold_in(streams_of[9], 71), 0)
    lengths = draw_lengths(jax.random.fold_in(streams_of[9], 71), 0)
    moved_slots = draw_moved_slots(jax.random.fold_in(streams_of[9], 71), 0)
    partner_mask = place_ends(jax.random.randint(streams_of[8], (MOVE,), 1, INSTANCES), jax.random.fold_in(streams_of[8], 1), 1, INSTANCES - 1).astype(jnp.int32)
    return dict(x_steps=x_steps, norm_gain=norm_gain, w_query=w_query, w_keyval=w_keyval, w_out=w_out, key_cache=key_cache, lengths=lengths, moved_slots=moved_slots, partner_mask=partner_mask)


eps_norm = 1e-05
rope_base = 500000.0
floor_score = -1e+30

def rotary(vectors, positions):
    half_dim = vectors.shape[-1] // 2
    frequency = rope_base ** (-(jnp.arange(half_dim, dtype=jnp.float32) * 2.0) / vectors.shape[-1])
    angles = positions.astype(jnp.float32)[..., None] * frequency
    cosine = jnp.cos(angles)[..., None, :]
    sine_part = jnp.sin(angles)[..., None, :]
    first_half = vectors[..., :half_dim]
    second_half = vectors[..., half_dim:]
    return jnp.concatenate([first_half * cosine - second_half * sine_part, second_half * cosine + first_half * sine_part], -1)

def block_terms(grouped, block, start, length_rows):
    queries = grouped.astype(jnp.float32)
    keys = block[..., :HD].astype(jnp.float32)
    values = block[..., HD:].astype(jnp.float32)
    scores = jnp.einsum('irkgd,irktd->irkgt', queries, keys) / math.sqrt(HD)
    places = start + jnp.arange(BLK, dtype=jnp.int32)
    visible = (places[None, None, :] < length_rows[:, :, None])[:, :, None, None, :]
    scores = jnp.where(visible, scores, floor_score)
    block_max = lax.optimization_barrier(jnp.max(scores, -1))
    weights = jnp.where(visible, jnp.exp(scores - block_max[..., None]), 0.0).astype(jnp.bfloat16)
    block_sum = lax.optimization_barrier(jnp.sum(weights.astype(jnp.float32), -1))
    block_mix = jnp.einsum('irkgt,irktd->irkgd', weights.astype(jnp.float32), values)
    return (block_max, block_sum, block_mix)

def fresh_terms(grouped, fresh_kv):
    queries = grouped.astype(jnp.float32)
    score = jnp.einsum('irkgd,irkd->irkg', queries, fresh_kv[..., :HD].astype(jnp.float32)) / math.sqrt(HD)
    block_mix = jnp.broadcast_to(fresh_kv[:, :, :, None, HD:].astype(jnp.float32), queries.shape)
    return (score, jnp.ones_like(score), block_mix)

def combine(pieces):
    overall_max = reduce(jnp.maximum, [piece[0] for piece in pieces])
    numerator = reduce(jnp.add, [jnp.exp(piece[0] - overall_max)[..., None] * piece[2] for piece in pieces])
    denominator = reduce(jnp.add, [jnp.exp(piece[0] - overall_max) * piece[1] for piece in pieces])
    return numerator / denominator[..., None]

def reference(x_steps, norm_gain, w_query, w_keyval, w_out, key_cache, lengths, moved_slots, partner_mask):
    inst_count = INSTANCES
    x_all = x_steps.reshape(2, inst_count, REQ, D)
    cache_all = key_cache.reshape(inst_count, REQ, N_TP, BLK, 2 * HD)
    length_all = lengths.reshape(inst_count, REQ)

    def project(step_x, positions):
        widened = step_x.astype(jnp.float32)
        normed = (widened * jax.lax.rsqrt(lax.optimization_barrier(jnp.mean(widened * widened, -1, keepdims=True)) + eps_norm) * norm_gain).astype(jnp.bfloat16)
        flat = normed.reshape(inst_count * REQ, D)
        query_raw = jnp.dot(flat, w_query, preferred_element_type=jnp.float32).reshape(inst_count, REQ, HEADS, HD)
        keyval_raw = jnp.dot(flat, w_keyval, preferred_element_type=jnp.float32).reshape(inst_count, REQ, KVH, 2, HD)
        queries = rotary(query_raw, positions).astype(jnp.bfloat16)
        keys = rotary(keyval_raw[..., 0, :], positions)
        fresh_kv = jnp.concatenate([keys, keyval_raw[..., 1, :]], -1).astype(jnp.bfloat16)
        return (queries, fresh_kv)

    def attend(queries, cache_rows, length_rows, fresh_list):
        grouped = queries.reshape(inst_count, REQ, KVH, HEADS // KVH, HD)
        blocks = cache_rows.reshape(inst_count, REQ, KVH, GROUP, BLK, 2 * HD)
        pieces = []
        for block_index in range(GROUP):
            pieces.append(block_terms(grouped, blocks[:, :, :, block_index], block_index * BLK, length_rows))
        for fresh_item in fresh_list:
            pieces.append(fresh_terms(grouped, fresh_item))
        attended = combine(pieces).reshape(inst_count * REQ, HEADS * HD).astype(jnp.bfloat16)
        return jnp.dot(attended, w_out, preferred_element_type=jnp.float32).astype(jnp.bfloat16)
    first_queries, first_fresh = project(x_all[0], length_all)
    first_out = attend(first_queries, cache_all, length_all, [first_fresh])
    row_ids = jnp.arange(inst_count, dtype=jnp.int32)[:, None]
    move_ids = jnp.arange(MOVE, dtype=jnp.int32)[None, :]
    partner = jnp.bitwise_xor(row_ids, partner_mask[None, :])
    slots_partner = moved_slots[partner, move_ids]
    arrived_rows = cache_all[partner, slots_partner]
    cache_next = cache_all.at[row_ids, moved_slots].set(arrived_rows)
    fresh_next = first_fresh.at[row_ids, moved_slots].set(first_fresh[partner, slots_partner])
    length_next = length_all.at[row_ids, moved_slots].set(length_all[partner, slots_partner])
    second_queries, second_fresh = project(x_all[1], length_next + 1)
    second_out = attend(second_queries, cache_next, length_next, [fresh_next, second_fresh])
    return (jnp.stack([first_out, second_out]), arrived_rows.reshape(inst_count * MOVE, N_TP, BLK, 2 * HD))
```

```python
import functools
import math

import jax
import jax.numpy as jnp
from jax import lax
from jax.experimental import pallas as pl
from jax.experimental.pallas import tpu as pltpu
from jax.sharding import PartitionSpec as P

BF = jnp.bfloat16
F32 = jnp.float32
EPS = 1e-05
ROPE_BASE = 500000.0
FLOOR = -1e30
HD = 128
BLK = 128
REQ = 64
HEADS = 8
SHARD = 512
CHIPS = 8
MOVE = 8
QW = HEADS * HD
PW = QW + 2 * HD + HD
ANY = pl.BlockSpec(memory_space=pl.ANY)
VMEM = pl.BlockSpec(memory_space=pltpu.VMEM)
SMEM = pl.BlockSpec(memory_space=pltpu.SMEM)
LIMIT = 48 * 1024 * 1024


def call(body, ins, outs, scratch, out_shapes, flops, moved):
    return pl.pallas_call(
        body,
        out_shape=out_shapes,
        in_specs=ins,
        out_specs=outs,
        scratch_shapes=scratch,
        compiler_params=pltpu.CompilerParams(vmem_limit_bytes=LIMIT),
        cost_estimate=pl.CostEstimate(flops=flops, bytes_accessed=moved, transcendentals=0),
    )


def shape(dims, kind):
    return jax.ShapeDtypeStruct(dims, kind)


def swap(value, axis, mask):
    count = lax.axis_size(axis)
    return lax.ppermute(value, axis, [(i, i ^ mask) for i in range(count)])


def pick_qkv(where, wq, wkv, wq_out, wkv_out, sems):
    other = 1 - where[0] % 2
    copies = []
    for b in range(CHIPS):
        rows = pl.ds(pl.multiple_of((2 * b + other) * SHARD, SHARD), SHARD)
        copies.append(pltpu.make_async_copy(wq.at[rows, :], wq_out.at[b], sems.at[2 * b]))
        copies.append(pltpu.make_async_copy(wkv.at[rows, :], wkv_out.at[b], sems.at[2 * b + 1]))
    for copy in copies:
        copy.start()
    for copy in copies:
        copy.wait()


def pick_out(where, wo, wo_out, sems):
    other = 1 - where[0] % 2
    copies = []
    for b in range(CHIPS):
        cols = pl.ds(pl.multiple_of((2 * b + other) * SHARD, SHARD), SHARD)
        copies.append(pltpu.make_async_copy(wo.at[:, cols], wo_out.at[b], sems.at[b]))
    for copy in copies:
        copy.start()
    for copy in copies:
        copy.wait()


def pick_rows(slots, cache, rows_a, rows_b, sems):
    half = MOVE // 2
    copies = []
    for j in range(MOVE):
        out = rows_a.at[j] if j < half else rows_b.at[j - half]
        copies.append(pltpu.make_async_copy(cache.at[slots[j]], out, sems.at[j]))
    for copy in copies:
        copy.start()
    for copy in copies:
        copy.wait()


def project(where, *refs):
    xs = refs[:CHIPS]
    gain, wq, wkv, wqs, wkvs, out, buf, acc, sems = refs[CHIPS:]
    me = where[0]
    core = me % 2
    pending = []
    for i in range(CHIPS):
        src = me ^ (2 * i)
        rows = pl.ds(pl.multiple_of(src * SHARD, SHARD), SHARD)
        group = [
            pltpu.make_async_copy(wq.at[rows, :], buf.at[i, :, pl.ds(0, SHARD)], sems.at[i, 0]),
            pltpu.make_async_copy(wqs.at[src // 2], buf.at[i, :, pl.ds(SHARD, SHARD)], sems.at[i, 1]),
            pltpu.make_async_copy(wkv.at[rows, :], buf.at[i, :, pl.ds(QW, HD)], sems.at[i, 2]),
            pltpu.make_async_copy(wkvs.at[src // 2], buf.at[i, :, pl.ds(QW + HD, HD)], sems.at[i, 3]),
        ]
        for copy in group:
            copy.start()
        pending.append(group)
    squares = None
    for i in range(CHIPS):
        src = me ^ (2 * i)
        wide = xs[i][...].astype(F32)
        scaled = (wide * gain[pl.ds(src, 1), :]).astype(BF)
        sq = wide * wide
        part = sq[:, :HD] + sq[:, HD : 2 * HD] + sq[:, 2 * HD : 3 * HD] + sq[:, 3 * HD :]
        squares = part if squares is None else squares + part
        for copy in pending[i]:
            copy.wait()
        term = jnp.dot(scaled, buf[i], preferred_element_type=F32)
        if i == 0:
            acc[...] = term
        else:
            acc[...] += term
    mine = core * SHARD
    theirs = SHARD - mine
    out[:, pl.ds(pl.multiple_of(mine, SHARD), SHARD)] = acc[:, :SHARD]
    out[:, pl.ds(pl.multiple_of(theirs, SHARD), SHARD)] = acc[:, SHARD:QW]
    out[:, pl.ds(pl.multiple_of(QW + core * HD, HD), HD)] = acc[:, QW : QW + HD]
    out[:, pl.ds(pl.multiple_of(QW + HD - core * HD, HD), HD)] = acc[:, QW + HD :]
    out[:, pl.ds(QW + 2 * HD, HD)] = squares


def softmax_pair(q_pair, keys, values, len_a, len_b):
    rows = q_pair.shape[0]
    half = rows // 2
    scores = lax.dot_general(
        q_pair, keys, (((1,), (1,)), ((), ())), preferred_element_type=F32
    ) * (1.0 / math.sqrt(HD))
    lane = lax.broadcasted_iota(jnp.int32, (rows, 2 * BLK), 1)
    upper = lax.broadcasted_iota(jnp.int32, (rows, 2 * BLK), 0) >= half
    low = jnp.where(upper, BLK, 0)
    high = jnp.where(upper, BLK + len_b, len_a)
    visible = jnp.logical_and(lane >= low, lane < high)
    scores = jnp.where(visible, scores, FLOOR)
    top = jnp.max(scores, -1, keepdims=True)
    weights = jnp.where(visible, jnp.exp(scores - top), 0.0).astype(BF)
    total = jnp.sum(weights.astype(F32), -1, keepdims=True)
    mix = jnp.dot(weights, values, preferred_element_type=F32)
    return top, total, mix


def attend(step, moving, where, lens, slots, *refs):
    if moving:
        mine, recv, cosine, sine, cache, arr_a, arr_b, terms, q_out, fresh_out, kv, arr, wide, sems = refs
    else:
        mine, recv, cosine, sine, cache, terms, q_out, fresh_out, sent_out, kv, wide, sems = refs
    core = where[0] % 2
    base = core * BLK
    chunks = 4
    per = REQ // chunks
    copies = []
    for i in range(chunks):
        copies.append(
            pltpu.make_async_copy(cache.at[pl.ds(i * per, per)], kv.at[pl.ds(i * per, per)], sems.at[i])
        )
    if moving:
        half = MOVE // 2
        copies.append(pltpu.make_async_copy(arr_a, arr.at[pl.ds(0, half)], sems.at[chunks]))
        copies.append(pltpu.make_async_copy(arr_b, arr.at[pl.ds(half, half)], sems.at[chunks + 1]))
    for copy in copies:
        copy.start()
    rows = pl.ds(step * REQ, REQ)
    squares = mine[rows, pl.ds(QW + 2 * HD, HD)] + recv[rows, pl.ds(QW + 2 * HD, HD)]
    mean = jnp.sum(squares, -1, keepdims=True) * (1.0 / (2 * CHIPS * SHARD))
    scale = lax.rsqrt(mean + EPS)
    cos = cosine[...]
    sin = sine[...]

    def taken(col):
        return (mine[rows, pl.ds(col, HD)] + recv[rows, pl.ds(col, HD)]) * scale

    def turned(vec):
        return vec * cos + pltpu.roll(vec, HD // 2, 1) * sin

    for h in range(HEADS):
        q_out[pl.ds(h, REQ, stride=HEADS), :] = turned(taken(h * HD)).astype(BF).astype(F32)
    key = turned(taken(QW)).astype(BF).astype(F32)
    value = taken(QW + HD).astype(BF).astype(F32)
    wide[:, pl.ds(0, HD)] = key
    wide[:, pl.ds(HD, HD)] = value
    fresh_out[...] = wide[...]
    if not moving:
        for j in range(MOVE):
            sent_out[pl.ds(j, 1), :] = wide[pl.ds(slots[j], 1), :]

    lane8 = lax.broadcasted_iota(jnp.int32, (HEADS, HD), 1)

    def noted(stats, slot, top, total):
        stats = jnp.where(lane8 == slot, top, stats)
        return jnp.where(lane8 == slot + REQ, total, stats)

    def clipped(length):
        return jnp.clip(length - base, 0, BLK)

    def pair(p, stats):
        q_pair = q_out[pl.ds(pl.multiple_of(p * 2 * HEADS, 2 * HEADS), 2 * HEADS), :].astype(BF)
        block = kv[pl.ds(2 * p, 2)].reshape(2 * BLK, 2 * HD)
        top, total, mix = softmax_pair(
            q_pair, block[:, :HD], block[:, HD:], clipped(lens[2 * p]), clipped(lens[2 * p + 1])
        )
        terms[pl.ds(pl.multiple_of(p * 2 * HEADS, 2 * HEADS), 2 * HEADS), :] = mix
        stats = noted(stats, 2 * p, top[:HEADS], total[:HEADS])
        return noted(stats, 2 * p + 1, top[HEADS:], total[HEADS:])

    stats = jnp.zeros((HEADS, HD), F32)
    for i in range(chunks):
        copies[i].wait()
        stats = lax.fori_loop(i * per // 2, (i + 1) * per // 2, pair, stats, unroll=True)
    if moving:
        copies[chunks].wait()
        copies[chunks + 1].wait()
        for p in range(MOVE // 2):
            one, two = slots[2 * p], slots[2 * p + 1]
            at_one = pl.ds(pl.multiple_of(one * HEADS, HEADS), HEADS)
            at_two = pl.ds(pl.multiple_of(two * HEADS, HEADS), HEADS)
            q_pair = jnp.concatenate([q_out[at_one, :], q_out[at_two, :]], 0).astype(BF)
            block = arr[pl.ds(2 * p, 2)].reshape(2 * BLK, 2 * HD)
            top, total, mix = softmax_pair(
                q_pair, block[:, :HD], block[:, HD:], clipped(lens[one]), clipped(lens[two])
            )
            terms[at_one, :] = mix[:HEADS]
            terms[at_two, :] = mix[HEADS:]
            stats = noted(stats, one, top[:HEADS], total[:HEADS])
            stats = noted(stats, two, top[HEADS:], total[HEADS:])
    terms[pl.ds(REQ * HEADS, HEADS), :] = stats


def finish(where, slots, *refs):
    (t1m, t1r, q1, f1, t2m, t2r, q2, f2, came, wo, wos) = refs[:11]
    outs = refs[11 : 11 + CHIPS]
    own_buf, sib_buf, carried, flat, att, sems = refs[11 + CHIPS :]
    me = where[0]
    core = me % 2
    pending = []
    for i in range(CHIPS):
        k = 8 + 2 * i if i < 4 else 2 * (i - 4)
        dst = me ^ k
        cols = pl.ds(pl.multiple_of(dst * SHARD, SHARD), SHARD)
        group = [
            pltpu.make_async_copy(wo.at[:, cols], own_buf.at[i], sems.at[i, 0]),
            pltpu.make_async_copy(wos.at[dst // 2], sib_buf.at[i], sems.at[i, 1]),
        ]
        for copy in group:
            copy.start()
        pending.append(group)
    carried[...] = f1[...]
    for j in range(MOVE):
        carried[pl.ds(slots[j], 1), :] = came[pl.ds(j, 1), :]

    def combine(step, mine, recv, q, fresh):
        stats_m = mine[pl.ds(REQ * HEADS, HEADS), :]
        stats_r = recv[pl.ds(REQ * HEADS, HEADS), :]
        for r in range(REQ):
            at = pl.ds(r * HEADS, HEADS)
            query = q[at, :]
            tops = [stats_m[:, r : r + 1], stats_r[:, r : r + 1]]
            sums = [stats_m[:, r + REQ : r + REQ + 1], stats_r[:, r + REQ : r + REQ + 1]]
            mixes = [mine[at, :], recv[at, :]]
            for row in fresh:
                key = row[pl.ds(r, 1), pl.ds(0, HD)]
                tops.append(jnp.sum(query * key, -1, keepdims=True) * (1.0 / math.sqrt(HD)))
                sums.append(None)
                mixes.append(row[pl.ds(r, 1), pl.ds(HD, HD)])
            overall = functools.reduce(jnp.maximum, tops)
            numerator = denominator = None
            for top, total, mix in zip(tops, sums, mixes):
                factor = jnp.exp(top - overall)
                low = factor if total is None else factor * total
                numerator = factor * mix if numerator is None else numerator + factor * mix
                denominator = low if denominator is None else denominator + low
            flat[at, :] = numerator / denominator
        for h in range(HEADS):
            att[pl.ds(step * REQ, REQ), pl.ds(h * HD, HD)] = flat[
                pl.ds(h, REQ, stride=HEADS), :
            ].astype(BF)

    combine(0, t1m, t1r, q1, [f1])
    combine(1, t2m, t2r, q2, [carried, f2])
    own = att[:, pl.ds(pl.multiple_of(core * SHARD, SHARD), SHARD)]
    sib = att[:, pl.ds(pl.multiple_of(SHARD - core * SHARD, SHARD), SHARD)]
    for i in range(CHIPS):
        for copy in pending[i]:
            copy.wait()
        outs[i][...] = (
            jnp.dot(own, own_buf[i], preferred_element_type=F32)
            + jnp.dot(sib, sib_buf[i], preferred_element_type=F32)
        ).astype(BF)


def shards(
    x_steps, norm_gain, w_query, w_keyval, w_out, key_cache, lengths, moved_slots, partner_mask
):
    dma = pltpu.SemaphoreType.DMA
    me = lax.axis_index("tp")
    instance = lax.axis_index("inst")
    where = jnp.reshape(me, (1,)).astype(jnp.int32)
    cache = key_cache[:, 0]

    own_x = x_steps.reshape(2 * REQ, SHARD)
    far_x = swap(own_x, "tp", 8)
    near = [own_x] + [swap(own_x, "tp", 2 * i) for i in (1, 2, 3)]
    far = [far_x] + [swap(far_x, "tp", 2 * i) for i in (1, 2, 3)]

    wq_send, wkv_send = call(
        pick_qkv,
        [SMEM, ANY, ANY],
        [ANY, ANY],
        [dma((2 * CHIPS,))],
        [shape((CHIPS, SHARD, SHARD), BF), shape((CHIPS, SHARD, HD), BF)],
        0,
        10 << 20,
    )(where, w_query, w_keyval)
    wqs = swap(wq_send, "tp", 1)
    wkvs = swap(wkv_send, "tp", 1)
    wo_send = call(
        pick_out,
        [SMEM, ANY],
        ANY,
        [dma((CHIPS,))],
        shape((CHIPS, SHARD, SHARD), BF),
        0,
        8 << 20,
    )(where, w_out)
    wos = swap(wo_send, "tp", 1)

    move_ids = jnp.arange(MOVE, dtype=jnp.int32)
    partner = jnp.bitwise_xor(instance, partner_mask)
    slots = lax.dynamic_index_in_dim(moved_slots, instance, 0, False)
    slots_partner = moved_slots[partner, move_ids]
    own_lengths = lax.dynamic_slice_in_dim(lengths, instance * REQ, REQ)
    next_lengths = own_lengths.at[slots].set(lengths[partner * REQ + slots_partner])
    half = MOVE // 2
    rows_a, rows_b = call(
        pick_rows,
        [SMEM, ANY],
        [ANY, ANY],
        [dma((MOVE,))],
        [shape((half, BLK, 2 * HD), BF)] * 2,
        0,
        1 << 20,
    )(slots, cache)

    def hop(part, bit, masks):
        took = ((masks >> bit) & 1 == 1).reshape((-1,) + (1,) * (part.ndim - 1))
        return jnp.where(took, swap(part, "inst", 1 << bit), part)

    for bit_a, bit_b in ((1, 2), (2, 0), (0, 1)):
        rows_a = hop(rows_a, bit_a, partner_mask[:half])
        rows_b = hop(rows_b, bit_b, partner_mask[half:])
    arrived = jnp.concatenate([rows_a, rows_b], 0)[:, None]

    def tables(positions):
        frequency = ROPE_BASE ** (-(jnp.arange(HD // 2, dtype=F32) * 2.0) / HD)
        angles = positions.astype(F32)[:, None] * frequency
        cos, sin = jnp.cos(angles), jnp.sin(angles)
        return jnp.concatenate([cos, cos], 1), jnp.concatenate([-sin, sin], 1)

    cos1, sin1 = tables(own_lengths)
    cos2, sin2 = tables(next_lengths + 1)

    rows = 2 * REQ
    proj = call(
        project,
        [SMEM] + [VMEM] * CHIPS + [VMEM] + [ANY] * 4,
        VMEM,
        [
            pltpu.VMEM((CHIPS, SHARD, QW + 2 * HD), BF),
            pltpu.VMEM((rows, QW + 2 * HD), F32),
            dma((CHIPS, 4)),
        ],
        shape((rows, PW), F32),
        2 * rows * CHIPS * SHARD * (QW + 2 * HD),
        12 << 20,
    )(where, *near, *far, norm_gain.reshape(2 * CHIPS, SHARD), w_query, w_keyval, wqs, wkvs)
    proj_sib = swap(proj, "tp", 1)

    term_shape = shape((REQ * HEADS + HEADS, HD), F32)
    q_shape = shape((REQ * HEADS, HD), F32)
    fresh_shape = shape((REQ, 2 * HD), F32)
    kv_scratch = pltpu.VMEM((REQ, BLK, 2 * HD), BF)
    wide_scratch = pltpu.VMEM((REQ, 2 * HD), F32)
    t1, q1, f1, sent = call(
        functools.partial(attend, 0, False),
        [SMEM] * 3 + [VMEM] * 4 + [ANY],
        [VMEM] * 4,
        [kv_scratch, wide_scratch, dma((4,))],
        [term_shape, q_shape, fresh_shape, shape((MOVE, 2 * HD), F32)],
        4 * REQ * HEADS * BLK * HD,
        6 << 20,
    )(where, own_lengths, slots, proj, proj_sib, cos1, sin1, cache)
    t1_sib = swap(t1, "tp", 1)
    came = sent.astype(BF)
    for bit in range(3):
        came = hop(came, bit, partner_mask)
    came = came.astype(F32)
    t2, q2, f2 = call(
        functools.partial(attend, 1, True),
        [SMEM] * 3 + [VMEM] * 4 + [ANY] * 3,
        [VMEM] * 3,
        [kv_scratch, pltpu.VMEM((MOVE, BLK, 2 * HD), BF), wide_scratch, dma((6,))],
        [term_shape, q_shape, fresh_shape],
        4 * REQ * HEADS * BLK * HD,
        6 << 20,
    )(where, next_lengths, slots, proj, proj_sib, cos2, sin2, cache, rows_a, rows_b)
    t2_sib = swap(t2, "tp", 1)

    parts = call(
        finish,
        [SMEM] * 2 + [VMEM] * 9 + [ANY] * 2,
        [VMEM] * CHIPS,
        [
            pltpu.VMEM((CHIPS, SHARD, SHARD), BF),
            pltpu.VMEM((CHIPS, SHARD, SHARD), BF),
            pltpu.VMEM((REQ, 2 * HD), F32),
            pltpu.VMEM((REQ * HEADS, HD), F32),
            pltpu.VMEM((rows, QW), BF),
            dma((CHIPS, 2)),
        ],
        [shape((rows, SHARD), BF)] * CHIPS,
        2 * rows * QW * CHIPS * SHARD,
        10 << 20,
    )(where, slots, t1, t1_sib, q1, f1, t2, t2_sib, q2, f2, came, w_out, wos)

    def added(values):
        return functools.reduce(jnp.add, [value.astype(F32) for value in values])

    other = added([parts[0]] + [swap(parts[i], "tp", 2 * i) for i in (1, 2, 3)]).astype(BF)
    crossed = swap(other, "tp", 8)
    same = added([parts[4]] + [swap(parts[4 + i], "tp", 2 * i) for i in (1, 2, 3)])
    out = (same + crossed.astype(F32)).astype(BF)
    return out.reshape(2, REQ, SHARD), arrived


def solution(mesh):
    placed = (
        P(None, "inst", "tp"),
        P(),
        P(None, "tp"),
        P(None, "tp"),
        P("tp", None),
        P("inst", "tp", None, None),
        P(),
        P(),
        P(),
    )
    return jax.shard_map(
        shards,
        mesh=mesh,
        in_specs=placed,
        out_specs=(P(None, "inst", "tp"), P("inst", "tp", None, None)),
        check_vma=False,
    )
```

```python
import functools
import math

import jax
import jax.numpy as jnp
from jax import lax
from jax.experimental import pallas as pl
from jax.experimental.pallas import tpu as pltpu
from jax.sharding import PartitionSpec as P

BF = jnp.bfloat16
F32 = jnp.float32
EPS = 1e-05
ROPE_BASE = 500000.0
FLOOR = -1e30
HD = 128
BLK = 128
REQ = 64
HEADS = 8
SHARD = 512
CHIPS = 8
MOVE = 8
QW = HEADS * HD
PW = QW + 2 * HD + HD
ANY = pl.BlockSpec(memory_space=pl.ANY)
VMEM = pl.BlockSpec(memory_space=pltpu.VMEM)
SMEM = pl.BlockSpec(memory_space=pltpu.SMEM)
LIMIT = 48 * 1024 * 1024


def call(body, ins, outs, scratch, out_shapes, flops, moved):
    return pl.pallas_call(
        body,
        out_shape=out_shapes,
        in_specs=ins,
        out_specs=outs,
        scratch_shapes=scratch,
        compiler_params=pltpu.CompilerParams(vmem_limit_bytes=LIMIT),
        cost_estimate=pl.CostEstimate(flops=flops, bytes_accessed=moved, transcendentals=0),
    )


def shape(dims, kind):
    return jax.ShapeDtypeStruct(dims, kind)


def swap(value, axis, mask):
    count = lax.axis_size(axis)
    return lax.ppermute(value, axis, [(i, i ^ mask) for i in range(count)])


def pick_qkv(where, wq, wkv, wq_out, wkv_out, sems):
    other = 1 - where[0] % 2
    copies = []
    for b in range(CHIPS):
        rows = pl.ds(pl.multiple_of((2 * b + other) * SHARD, SHARD), SHARD)
        copies.append(pltpu.make_async_copy(wq.at[rows, :], wq_out.at[b], sems.at[2 * b]))
        copies.append(pltpu.make_async_copy(wkv.at[rows, :], wkv_out.at[b], sems.at[2 * b + 1]))
    for copy in copies:
        copy.start()
    for copy in copies:
        copy.wait()


def pick_out(where, wo, wo_out, sems):
    other = 1 - where[0] % 2
    copies = []
    for b in range(CHIPS):
        cols = pl.ds(pl.multiple_of((2 * b + other) * SHARD, SHARD), SHARD)
        copies.append(pltpu.make_async_copy(wo.at[:, cols], wo_out.at[b], sems.at[b]))
    for copy in copies:
        copy.start()
    for copy in copies:
        copy.wait()


def pick_rows(slots, cache, rows_a, rows_b, sems):
    half = MOVE // 2
    copies = []
    for j in range(MOVE):
        out = rows_a.at[j] if j < half else rows_b.at[j - half]
        copies.append(pltpu.make_async_copy(cache.at[slots[j]], out, sems.at[j]))
    for copy in copies:
        copy.start()
    for copy in copies:
        copy.wait()


def project(where, *refs):
    xs = refs[:CHIPS]
    gain, wq, wkv, wqs, wkvs, out, buf, held, acc, sems = refs[CHIPS:]
    me = where[0]
    core = me % 2
    pending = []
    for i in range(CHIPS):
        src = me ^ (2 * i)
        rows = pl.ds(pl.multiple_of(src * SHARD, SHARD), SHARD)
        group = [
            pltpu.make_async_copy(xs[i], held.at[i], sems.at[i, 4]),
            pltpu.make_async_copy(wq.at[rows, :], buf.at[i, :, pl.ds(0, SHARD)], sems.at[i, 0]),
            pltpu.make_async_copy(wqs.at[src // 2], buf.at[i, :, pl.ds(SHARD, SHARD)], sems.at[i, 1]),
            pltpu.make_async_copy(wkv.at[rows, :], buf.at[i, :, pl.ds(QW, HD)], sems.at[i, 2]),
            pltpu.make_async_copy(wkvs.at[src // 2], buf.at[i, :, pl.ds(QW + HD, HD)], sems.at[i, 3]),
        ]
        for copy in group:
            copy.start()
        pending.append(group)
    squares = None
    for i in range(CHIPS):
        src = me ^ (2 * i)
        for copy in pending[i]:
            copy.wait()
        wide = held[i].astype(F32)
        scaled = (wide * gain[pl.ds(src, 1), :]).astype(BF)
        sq = wide * wide
        part = sq[:, :HD] + sq[:, HD : 2 * HD] + sq[:, 2 * HD : 3 * HD] + sq[:, 3 * HD :]
        squares = part if squares is None else squares + part
        term = jnp.dot(scaled, buf[i], preferred_element_type=F32)
        if i == 0:
            acc[...] = term
        else:
            acc[...] += term
    mine = core * SHARD
    theirs = SHARD - mine
    out[:, pl.ds(pl.multiple_of(mine, SHARD), SHARD)] = acc[:, :SHARD]
    out[:, pl.ds(pl.multiple_of(theirs, SHARD), SHARD)] = acc[:, SHARD:QW]
    out[:, pl.ds(pl.multiple_of(QW + core * HD, HD), HD)] = acc[:, QW : QW + HD]
    out[:, pl.ds(pl.multiple_of(QW + HD - core * HD, HD), HD)] = acc[:, QW + HD :]
    out[:, pl.ds(QW + 2 * HD, HD)] = squares


def block_terms(queries, blocks, lens):
    scores = []
    for p, block in enumerate(blocks):
        both = jnp.concatenate(queries[2 * p : 2 * p + 2], 0).astype(BF)
        pair = lax.dot_general(
            both, block[:, :HD], (((1,), (1,)), ((), ())), preferred_element_type=F32
        )
        scores += [pair[:HEADS, :BLK], pair[HEADS:, BLK:]]
    lane = lax.broadcasted_iota(jnp.int32, (HEADS, BLK), 1)
    visible = jnp.concatenate([(lane < length).astype(F32) for length in lens], 0) > 0.0
    scores = jnp.where(visible, jnp.concatenate(scores, 0) * (1.0 / math.sqrt(HD)), FLOOR)
    top = jnp.max(scores, -1, keepdims=True)
    weights = jnp.where(visible, jnp.exp(scores - top), 0.0).astype(BF).astype(F32)
    total = jnp.sum(weights, -1, keepdims=True)
    zero = jnp.zeros((HEADS, BLK), F32)
    mixes = []
    for p, block in enumerate(blocks):
        at = 2 * p * HEADS
        one, two = weights[at : at + HEADS], weights[at + HEADS : at + 2 * HEADS]
        both = jnp.concatenate(
            [jnp.concatenate([one, zero], 1), jnp.concatenate([zero, two], 1)], 0
        ).astype(BF)
        mixes.append(jnp.dot(both, block[:, HD:], preferred_element_type=F32))
    return top, total, mixes


def attend(step, moving, where, lens, slots, *refs):
    if moving:
        mine, recv, cosine, sine, cache, arr_a, arr_b, terms, q_out, fresh_out, kv, arr, wide, sems = refs
    else:
        mine, recv, cosine, sine, cache, terms, q_out, fresh_out, sent_out, kv, wide, sems = refs
    core = where[0] % 2
    base = core * BLK
    chunks = 4
    per = REQ // chunks
    copies = []
    for i in range(chunks):
        copies.append(
            pltpu.make_async_copy(cache.at[pl.ds(i * per, per)], kv.at[pl.ds(i * per, per)], sems.at[i])
        )
    if moving:
        half = MOVE // 2
        copies.append(pltpu.make_async_copy(arr_a, arr.at[pl.ds(0, half)], sems.at[chunks]))
        copies.append(pltpu.make_async_copy(arr_b, arr.at[pl.ds(half, half)], sems.at[chunks + 1]))
    for copy in copies:
        copy.start()
    rows = pl.ds(step * REQ, REQ)
    squares = mine[rows, pl.ds(QW + 2 * HD, HD)] + recv[rows, pl.ds(QW + 2 * HD, HD)]
    mean = jnp.sum(squares, -1, keepdims=True) * (1.0 / (2 * CHIPS * SHARD))
    scale = lax.rsqrt(mean + EPS)
    cos = cosine[...]
    sin = sine[...]

    def taken(col):
        return (mine[rows, pl.ds(col, HD)] + recv[rows, pl.ds(col, HD)]) * scale

    def turned(vec):
        return vec * cos + pltpu.roll(vec, HD // 2, 1) * sin

    for h in range(HEADS):
        q_out[pl.ds(h, REQ, stride=HEADS), :] = turned(taken(h * HD)).astype(BF).astype(F32)
    key = turned(taken(QW)).astype(BF).astype(F32)
    value = taken(QW + HD).astype(BF).astype(F32)
    wide[:, pl.ds(0, HD)] = key
    wide[:, pl.ds(HD, HD)] = value
    fresh_out[...] = wide[...]
    if not moving:
        for j in range(MOVE):
            sent_out[pl.ds(j, 1), :] = wide[pl.ds(slots[j], 1), :]

    lane8 = lax.broadcasted_iota(jnp.int32, (HEADS, HD), 1)

    def noted(stats, slot, top, total):
        stats = jnp.where(lane8 == slot, top, stats)
        return jnp.where(lane8 == slot + REQ, total, stats)

    def clipped(length):
        return jnp.clip(length - base, 0, BLK)

    stats = jnp.zeros((HEADS, HD), F32)
    for i in range(chunks):
        copies[i].wait()
        mine_r = range(i * per, (i + 1) * per)
        top, total, mixes = block_terms(
            [q_out[pl.ds(r * HEADS, HEADS), :] for r in mine_r],
            [kv[pl.ds(r, 2)].reshape(2 * BLK, 2 * HD) for r in mine_r[::2]],
            [clipped(lens[r]) for r in mine_r],
        )
        for j, r in enumerate(mine_r):
            at = slice(j * HEADS, (j + 1) * HEADS)
            stats = noted(stats, r, top[at], total[at])
            if j % 2 == 0:
                terms[pl.ds(r * HEADS, 2 * HEADS), :] = mixes[j // 2]
    if moving:
        copies[chunks].wait()
        copies[chunks + 1].wait()
        places = [pl.ds(pl.multiple_of(slots[j] * HEADS, HEADS), HEADS) for j in range(MOVE)]
        top, total, mixes = block_terms(
            [q_out[place, :] for place in places],
            [arr[pl.ds(j, 2)].reshape(2 * BLK, 2 * HD) for j in range(0, MOVE, 2)],
            [clipped(lens[slots[j]]) for j in range(MOVE)],
        )
        for j in range(MOVE):
            at = slice(j * HEADS, (j + 1) * HEADS)
            stats = noted(stats, slots[j], top[at], total[at])
            terms[places[j], :] = mixes[j // 2][(j % 2) * HEADS : (j % 2 + 1) * HEADS]
    terms[pl.ds(REQ * HEADS, HEADS), :] = stats


def finish(where, slots, *refs):
    (t1m, t1r, q1, f1, t2m, t2r, q2, f2, came, wo, wos) = refs[:11]
    outs = refs[11 : 11 + CHIPS]
    own_buf, sib_buf, carried, flat, att, sems = refs[11 + CHIPS :]
    me = where[0]
    core = me % 2
    pending = []
    for i in range(CHIPS):
        k = 8 + 2 * i if i < 4 else 2 * (i - 4)
        dst = me ^ k
        cols = pl.ds(pl.multiple_of(dst * SHARD, SHARD), SHARD)
        group = [
            pltpu.make_async_copy(wo.at[:, cols], own_buf.at[i], sems.at[i, 0]),
            pltpu.make_async_copy(wos.at[dst // 2], sib_buf.at[i], sems.at[i, 1]),
        ]
        for copy in group:
            copy.start()
        pending.append(group)
    carried[...] = f1[...]
    for j in range(MOVE):
        carried[pl.ds(slots[j], 1), :] = came[pl.ds(j, 1), :]

    lane = lax.broadcasted_iota(jnp.int32, (HEADS, REQ), 1)

    def combine(step, mine, recv, q, fresh):
        stats_m = mine[pl.ds(REQ * HEADS, HEADS), :]
        stats_r = recv[pl.ds(REQ * HEADS, HEADS), :]
        tops = [stats_m[:, :REQ], stats_r[:, :REQ]]
        sums = [stats_m[:, REQ:], stats_r[:, REQ:]]
        for row in fresh:
            keys = row[:, pl.ds(0, HD)].astype(BF)
            scores = lax.dot_general(
                q[...].astype(BF), keys, (((1,), (1,)), ((), ())), preferred_element_type=F32
            )
            taken = [
                jnp.where(lane == r, scores[r * HEADS : (r + 1) * HEADS], 0.0) for r in range(REQ)
            ]
            while len(taken) > 1:
                taken = [taken[i] + taken[i + 1] for i in range(0, len(taken), 2)]
            tops.append(taken[0] * (1.0 / math.sqrt(HD)))
            sums.append(1.0)
        overall = functools.reduce(jnp.maximum, tops)
        factors = [jnp.exp(top - overall) for top in tops]
        below = functools.reduce(jnp.add, [f * s for f, s in zip(factors, sums)])
        factors = [f / below for f in factors]
        for r in range(REQ):
            at = pl.ds(r * HEADS, HEADS)
            mixes = [mine[at, :], recv[at, :]] + [row[pl.ds(r, 1), pl.ds(HD, HD)] for row in fresh]
            flat[at, :] = functools.reduce(
                jnp.add, [f[:, r : r + 1] * mix for f, mix in zip(factors, mixes)]
            )
        for h in range(HEADS):
            att[pl.ds(step * REQ, REQ), pl.ds(h * HD, HD)] = flat[
                pl.ds(h, REQ, stride=HEADS), :
            ].astype(BF)

    combine(0, t1m, t1r, q1, [f1])
    combine(1, t2m, t2r, q2, [carried, f2])
    own = att[:, pl.ds(pl.multiple_of(core * SHARD, SHARD), SHARD)]
    sib = att[:, pl.ds(pl.multiple_of(SHARD - core * SHARD, SHARD), SHARD)]
    for i in range(CHIPS):
        for copy in pending[i]:
            copy.wait()
        outs[i][...] = (
            jnp.dot(own, own_buf[i], preferred_element_type=F32)
            + jnp.dot(sib, sib_buf[i], preferred_element_type=F32)
        ).astype(BF)


def shards(
    x_steps, norm_gain, w_query, w_keyval, w_out, key_cache, lengths, moved_slots, partner_mask
):
    dma = pltpu.SemaphoreType.DMA
    me = lax.axis_index("tp")
    instance = lax.axis_index("inst")
    where = jnp.reshape(me, (1,)).astype(jnp.int32)
    cache = key_cache[:, 0]

    own_x = x_steps.reshape(2 * REQ, SHARD)
    far_x = swap(own_x, "tp", 8)
    near = [own_x] + [swap(own_x, "tp", 2 * i) for i in (1, 2, 3)]
    far_x, where = lax.optimization_barrier((far_x, where))
    far = [far_x] + [swap(far_x, "tp", 2 * i) for i in (1, 2, 3)]

    wq_send, wkv_send = call(
        pick_qkv,
        [SMEM, ANY, ANY],
        [VMEM, VMEM],
        [dma((2 * CHIPS,))],
        [shape((CHIPS, SHARD, SHARD), BF), shape((CHIPS, SHARD, HD), BF)],
        0,
        10 << 20,
    )(where, w_query, w_keyval)
    wqs = swap(wq_send, "tp", 1)
    wkvs = swap(wkv_send, "tp", 1)
    wo_send = call(
        pick_out,
        [SMEM, ANY],
        VMEM,
        [dma((CHIPS,))],
        shape((CHIPS, SHARD, SHARD), BF),
        0,
        8 << 20,
    )(where, w_out)
    wos = swap(wo_send, "tp", 1)

    move_ids = jnp.arange(MOVE, dtype=jnp.int32)
    partner = jnp.bitwise_xor(instance, partner_mask)
    slots = lax.dynamic_index_in_dim(moved_slots, instance, 0, False)
    slots_partner = moved_slots[partner, move_ids]
    own_lengths = lax.dynamic_slice_in_dim(lengths, instance * REQ, REQ)
    next_lengths = own_lengths.at[slots].set(lengths[partner * REQ + slots_partner])
    half = MOVE // 2
    rows_a, rows_b = call(
        pick_rows,
        [SMEM, ANY],
        [VMEM, VMEM],
        [dma((MOVE,))],
        [shape((half, BLK, 2 * HD), BF)] * 2,
        0,
        1 << 20,
    )(slots, cache)

    def hop(part, bit, masks):
        took = ((masks >> bit) & 1 == 1).reshape((-1,) + (1,) * (part.ndim - 1))
        return jnp.where(took, swap(part, "inst", 1 << bit), part)

    for bit_a, bit_b in ((1, 2), (2, 0), (0, 1)):
        rows_a = hop(rows_a, bit_a, partner_mask[:half])
        rows_b = hop(rows_b, bit_b, partner_mask[half:])
    arrived = jnp.concatenate([rows_a, rows_b], 0)[:, None]

    def tables(positions):
        frequency = ROPE_BASE ** (-(jnp.arange(HD // 2, dtype=F32) * 2.0) / HD)
        angles = positions.astype(F32)[:, None] * frequency
        cos, sin = jnp.cos(angles), jnp.sin(angles)
        return jnp.concatenate([cos, cos], 1), jnp.concatenate([-sin, sin], 1)

    cos1, sin1 = tables(own_lengths)
    cos2, sin2 = tables(next_lengths + 1)

    rows = 2 * REQ
    proj = call(
        project,
        [SMEM] + [ANY] * CHIPS + [VMEM] + [ANY] * 4,
        VMEM,
        [
            pltpu.VMEM((CHIPS, SHARD, QW + 2 * HD), BF),
            pltpu.VMEM((CHIPS, rows, SHARD), BF),
            pltpu.VMEM((rows, QW + 2 * HD), F32),
            dma((CHIPS, 5)),
        ],
        shape((rows, PW), F32),
        2 * rows * CHIPS * SHARD * (QW + 2 * HD),
        12 << 20,
    )(where, *near, *far, norm_gain.reshape(2 * CHIPS, SHARD), w_query, w_keyval, wqs, wkvs)
    proj_sib = swap(proj, "tp", 1)

    term_shape = shape((REQ * HEADS + HEADS, HD), F32)
    q_shape = shape((REQ * HEADS, HD), F32)
    fresh_shape = shape((REQ, 2 * HD), F32)
    kv_scratch = pltpu.VMEM((REQ, BLK, 2 * HD), BF)
    wide_scratch = pltpu.VMEM((REQ, 2 * HD), F32)
    t1, q1, f1, sent = call(
        functools.partial(attend, 0, False),
        [SMEM] * 3 + [VMEM] * 4 + [ANY],
        [VMEM] * 4,
        [kv_scratch, wide_scratch, dma((4,))],
        [term_shape, q_shape, fresh_shape, shape((MOVE, 2 * HD), F32)],
        4 * REQ * HEADS * BLK * HD,
        6 << 20,
    )(where, own_lengths, slots, proj, proj_sib, cos1, sin1, cache)
    t1_sib = swap(t1, "tp", 1)
    came = sent.astype(BF)
    for bit in range(3):
        came = hop(came, bit, partner_mask)
    came = came.astype(F32)
    t2, q2, f2 = call(
        functools.partial(attend, 1, True),
        [SMEM] * 3 + [VMEM] * 4 + [ANY] * 3,
        [VMEM] * 3,
        [kv_scratch, pltpu.VMEM((MOVE, BLK, 2 * HD), BF), wide_scratch, dma((6,))],
        [term_shape, q_shape, fresh_shape],
        4 * REQ * HEADS * BLK * HD,
        6 << 20,
    )(where, next_lengths, slots, proj, proj_sib, cos2, sin2, cache, rows_a, rows_b)
    t2_sib = swap(t2, "tp", 1)

    parts = call(
        finish,
        [SMEM] * 2 + [VMEM] * 9 + [ANY] * 2,
        [VMEM] * CHIPS,
        [
            pltpu.VMEM((CHIPS, SHARD, SHARD), BF),
            pltpu.VMEM((CHIPS, SHARD, SHARD), BF),
            pltpu.VMEM((REQ, 2 * HD), F32),
            pltpu.VMEM((REQ * HEADS, HD), F32),
            pltpu.VMEM((rows, QW), BF),
            dma((CHIPS, 2)),
        ],
        [shape((rows, SHARD), BF)] * CHIPS,
        2 * rows * QW * CHIPS * SHARD,
        10 << 20,
    )(where, slots, t1, t1_sib, q1, f1, t2, t2_sib, q2, f2, came, w_out, wos)

    def added(values):
        return functools.reduce(jnp.add, [value.astype(F32) for value in values])

    other = added([parts[0]] + [swap(parts[i], "tp", 2 * i) for i in (1, 2, 3)]).astype(BF)
    crossed = swap(other, "tp", 8)
    same = added([parts[4]] + [swap(parts[4 + i], "tp", 2 * i) for i in (1, 2, 3)])
    out = (same + crossed.astype(F32)).astype(BF)
    return out.reshape(2, REQ, SHARD), arrived


def solution(mesh):
    placed = (
        P(None, "inst", "tp"),
        P(),
        P(None, "tp"),
        P(None, "tp"),
        P("tp", None),
        P("inst", "tp", None, None),
        P(),
        P(),
        P(),
    )
    return jax.shard_map(
        shards,
        mesh=mesh,
        in_specs=placed,
        out_specs=(P(None, "inst", "tp"), P("inst", "tp", None, None)),
        check_vma=False,
    )
```

```python
import functools
import math

import jax
import jax.numpy as jnp
import numpy as np
from jax import lax
from jax.experimental import pallas as pl
from jax.experimental.pallas import tpu as pltpu
from jax.sharding import PartitionSpec as P

BF = jnp.bfloat16
F32 = jnp.float32
EPS = 1e-05
ROPE_BASE = 500000.0
FLOOR = -1e30
HD = 128
BLK = 128
REQ = 64
HEADS = 8
SHARD = 512
CHIPS = 8
MOVE = 8
QW = HEADS * HD
OWN = SHARD + HD
ANY = pl.BlockSpec(memory_space=pl.ANY)
VMEM = pl.BlockSpec(memory_space=pltpu.VMEM)
SMEM = pl.BlockSpec(memory_space=pltpu.SMEM)
MIB = 1024 * 1024


def call(body, ins, outs, scratch, out_shapes, flops, moved, limit=48):
    return pl.pallas_call(
        body,
        out_shape=out_shapes,
        in_specs=ins,
        out_specs=outs,
        scratch_shapes=scratch,
        compiler_params=pltpu.CompilerParams(vmem_limit_bytes=limit * MIB),
        cost_estimate=pl.CostEstimate(flops=flops, bytes_accessed=moved, transcendentals=0),
    )


def shape(dims, kind):
    return jax.ShapeDtypeStruct(dims, kind)


def swap(value, axis, mask):
    count = lax.axis_size(axis)
    return lax.ppermute(value, axis, [(i, i ^ mask) for i in range(count)])


def prepare(
    where, moved, masks, lengths, frequency, cache, wo,
    slots, own_lens, next_lens, tables, rows, wo_out, held, angle, sems, row_sems,
):
    other = 1 - where[0] % 2
    instance = where[1]
    row_copies = [
        pltpu.make_async_copy(cache.at[moved[instance, j]], rows.at[j], row_sems.at[j])
        for j in range(MOVE)
    ]
    reads = []
    writes = []
    for b in range(CHIPS):
        cols = pl.ds(pl.multiple_of((2 * b + other) * SHARD, SHARD), SHARD)
        reads.append(pltpu.make_async_copy(wo.at[:, cols], held.at[b], sems.at[b, 0]))
        writes.append(pltpu.make_async_copy(held.at[b], wo_out.at[b], sems.at[b, 1]))
    for copy in reads + row_copies:
        copy.start()
    for r in range(REQ):
        length = lengths[instance * REQ + r]
        own_lens[r] = length
        next_lens[r] = length
        angle[pl.ds(r, 1), :] = jnp.full((1, HD), length.astype(F32))
        angle[pl.ds(REQ + r, 1), :] = jnp.full((1, HD), (length + 1).astype(F32))
    for j in range(MOVE):
        slot = moved[instance, j]
        partner = instance ^ masks[j]
        length = lengths[partner * REQ + moved[partner, j]]
        slots[j] = slot
        next_lens[slot] = length
        angle[pl.ds(REQ + slot, 1), :] = jnp.full((1, HD), (length + 1).astype(F32))
    turn = angle[...] * frequency[...]
    low = lax.broadcasted_iota(jnp.int32, turn.shape, 1) < HD // 2
    wave = jnp.sin(turn)
    tables[0] = jnp.cos(turn)
    tables[1] = jnp.where(low, -wave, wave)
    for read, write in zip(reads, writes):
        read.wait()
        write.start()
    for copy in row_copies + writes:
        copy.wait()


def project(where, slots, *refs):
    near, (near_sib,) = refs[: CHIPS // 2], refs[CHIPS // 2 : CHIPS // 2 + 1]
    far, (far_sib,) = refs[CHIPS // 2 + 1 : CHIPS + 1], refs[CHIPS + 1 : CHIPS + 2]
    gain, wq, wkv, tables, out, sent, acc, wide = refs[CHIPS + 2 :]
    me = where[0]
    half = CHIPS // 2
    squares = None
    for i in range(2 * CHIPS):
        src = me ^ (2 * (i % half) + (0, 1, 8, 9)[i // half])
        rows = pl.ds(pl.multiple_of(src * SHARD, SHARD), SHARD)
        ref = (near[i % half], near_sib, far[i % half], far_sib)[i // half]
        x = (ref[i % half] if i // half % 2 else ref[...]).astype(F32)
        scaled = (x * gain[pl.ds(src, 1), :]).astype(BF)
        sq = x * x
        part = sq[:, :HD] + sq[:, HD : 2 * HD] + sq[:, 2 * HD : 3 * HD] + sq[:, 3 * HD :]
        squares = part if squares is None else squares + part
        for at, weight in ((pl.ds(0, SHARD), wq), (pl.ds(SHARD, HD), wkv)):
            term = jnp.dot(scaled, weight[rows, :], preferred_element_type=F32)
            if i == 0:
                acc[:, at] = term
            else:
                acc[:, at] += term
    mean = jnp.sum(squares, -1, keepdims=True) * (1.0 / (2 * CHIPS * SHARD))
    scale = lax.rsqrt(mean + EPS)
    cos = tables[0]
    sin = tables[1]

    def turned(vec):
        return vec * cos + pltpu.roll(vec, HD // 2, 1) * sin

    for h in range(SHARD // HD):
        at = pl.ds(h * HD, HD)
        out[:, at] = turned(acc[:, at] * scale).astype(BF)
    raw = acc[:, pl.ds(SHARD, HD)] * scale
    kept = jnp.where(me % 2 == 0, turned(raw), raw).astype(BF)
    out[:, pl.ds(SHARD, HD)] = kept
    wide[...] = kept.astype(F32)
    sent[...] = jnp.zeros_like(sent)
    for j in range(MOVE):
        sent[pl.ds(j, 1), :] = wide[pl.ds(slots[j], 1), :]


def block_terms(queries, blocks, lens):
    scores = []
    for p, block in enumerate(blocks):
        both = jnp.concatenate(queries[2 * p : 2 * p + 2], 0).astype(BF)
        pair = lax.dot_general(
            both, block[:, :HD], (((1,), (1,)), ((), ())), preferred_element_type=F32
        )
        scores += [pair[:HEADS, :BLK], pair[HEADS:, BLK:]]
    lane = lax.broadcasted_iota(jnp.int32, (HEADS, BLK), 1)
    visible = jnp.concatenate([(lane < length).astype(F32) for length in lens], 0) > 0.0
    scores = jnp.where(visible, jnp.concatenate(scores, 0) * (1.0 / math.sqrt(HD)), FLOOR)
    top = jnp.max(scores, -1, keepdims=True)
    weights = jnp.where(visible, jnp.exp(scores - top), 0.0).astype(BF).astype(F32)
    total = jnp.sum(weights, -1, keepdims=True)
    zero = jnp.zeros((HEADS, BLK), F32)
    mixes = []
    for p, block in enumerate(blocks):
        at = 2 * p * HEADS
        one, two = weights[at : at + HEADS], weights[at + HEADS : at + 2 * HEADS]
        both = jnp.concatenate(
            [jnp.concatenate([one, zero], 1), jnp.concatenate([zero, two], 1)], 0
        ).astype(BF)
        mixes.append(jnp.dot(both, block[:, HD:], preferred_element_type=F32))
    return top, total, mixes


def noted(stats, slot, top, total):
    lane = lax.broadcasted_iota(jnp.int32, (HEADS, HD), 1)
    stats = jnp.where(lane == slot, top, stats)
    return jnp.where(lane == slot + REQ, total, stats)


def attend(step, where, lens, mine, recv, cache, terms, q_out, fresh_out, kv, sems):
    core = where[0] % 2
    base = core * BLK
    chunks = 4
    per = REQ // chunks
    copies = []
    for i in range(chunks):
        copies.append(
            pltpu.make_async_copy(cache.at[pl.ds(i * per, per)], kv.at[pl.ds(i * per, per)], sems.at[i])
        )
    for copy in copies:
        copy.start()
    rows = pl.ds(step * REQ, REQ)
    first = core == 0
    own = HEADS // 2

    def either(low_core, col):
        one = mine[rows, pl.ds(col, HD)].astype(F32)
        two = recv[rows, pl.ds(col, HD)].astype(F32)
        return jnp.where(first, one, two) if low_core else jnp.where(first, two, one)

    for h in range(HEADS):
        q_out[pl.ds(h, REQ, stride=HEADS), :] = either(h < own, (h % own) * HD)
    fresh_out[:, pl.ds(0, HD)] = either(True, SHARD)
    fresh_out[:, pl.ds(HD, HD)] = either(False, SHARD)

    stats = jnp.zeros((HEADS, HD), F32)
    for i in range(chunks):
        copies[i].wait()
        mine_r = range(i * per, (i + 1) * per)
        top, total, mixes = block_terms(
            [q_out[pl.ds(r * HEADS, HEADS), :] for r in mine_r],
            [kv[pl.ds(r, 2)].reshape(2 * BLK, 2 * HD) for r in mine_r[::2]],
            [jnp.clip(lens[r] - base, 0, BLK) for r in mine_r],
        )
        for j, r in enumerate(mine_r):
            at = slice(j * HEADS, (j + 1) * HEADS)
            stats = noted(stats, r, top[at], total[at])
            if j % 2 == 0:
                terms[pl.ds(r * HEADS, 2 * HEADS), :] = mixes[j // 2]
    terms[pl.ds(REQ * HEADS, HEADS), :] = stats


def attend_arrived(where, lens, slots, q, arrived, terms):
    base = where[0] % 2 * BLK
    top, total, mixes = block_terms(
        [q[pl.ds(pl.multiple_of(slots[j] * HEADS, HEADS), HEADS), :] for j in range(MOVE)],
        [arrived[pl.ds(j, 2)].reshape(2 * BLK, 2 * HD) for j in range(0, MOVE, 2)],
        [jnp.clip(lens[slots[j]] - base, 0, BLK) for j in range(MOVE)],
    )
    stats = jnp.zeros((HEADS, HD), F32)
    for j in range(MOVE):
        at = slice(j * HEADS, (j + 1) * HEADS)
        stats = noted(stats, j, top[at], total[at])
        if j % 2 == 0:
            terms[pl.ds(j * HEADS, 2 * HEADS), :] = mixes[j // 2]
    terms[pl.ds(MOVE * HEADS, HEADS), :] = stats


def attended(mine, recv, q, fresh, flat, att):
    lane = lax.broadcasted_iota(jnp.int32, (HEADS, REQ), 1)
    stats_m = mine[pl.ds(REQ * HEADS, HEADS), :]
    stats_r = recv[pl.ds(REQ * HEADS, HEADS), :]
    tops = [stats_m[:, :REQ], stats_r[:, :REQ]]
    sums = [stats_m[:, REQ:], stats_r[:, REQ:]]
    for row in fresh:
        keys = row[:, pl.ds(0, HD)].astype(BF)
        scores = lax.dot_general(
            q[...].astype(BF), keys, (((1,), (1,)), ((), ())), preferred_element_type=F32
        )
        taken = [
            jnp.where(lane == r, scores[r * HEADS : (r + 1) * HEADS], 0.0) for r in range(REQ)
        ]
        while len(taken) > 1:
            taken = [taken[i] + taken[i + 1] for i in range(0, len(taken), 2)]
        tops.append(taken[0] * (1.0 / math.sqrt(HD)))
        sums.append(1.0)
    overall = functools.reduce(jnp.maximum, tops)
    factors = [jnp.exp(top - overall) for top in tops]
    below = functools.reduce(jnp.add, [f * s for f, s in zip(factors, sums)])
    factors = [f / below for f in factors]
    for r in range(REQ):
        at = pl.ds(r * HEADS, HEADS)
        mixes = [mine[at, :], recv[at, :]] + [row[pl.ds(r, 1), pl.ds(HD, HD)] for row in fresh]
        flat[at, :] = functools.reduce(
            jnp.add, [f[:, r : r + 1] * mix for f, mix in zip(factors, mixes)]
        )
    for h in range(HEADS):
        att[:, pl.ds(h * HD, HD)] = flat[
            pl.ds(h, REQ, stride=HEADS), :
        ].astype(BF)


def out_copies(where, blocks, wo, wos, own_buf, sib_buf, sems):
    me = where[0]
    pending = []
    for n, i in enumerate(blocks):
        dst = me ^ (8 + 2 * i if i < 4 else 2 * (i - 4))
        cols = pl.ds(pl.multiple_of(dst * SHARD, SHARD), SHARD)
        group = [
            pltpu.make_async_copy(wo.at[:, cols], own_buf.at[n], sems.at[n, 0]),
            pltpu.make_async_copy(wos.at[dst // 2], sib_buf.at[n], sems.at[n, 1]),
        ]
        for copy in group:
            copy.start()
        pending.append(group)
    return pending


def out_blocks(where, att, pending, own_buf, sib_buf):
    core = where[0] % 2
    own = att[:, pl.ds(pl.multiple_of(core * SHARD, SHARD), SHARD)]
    sib = att[:, pl.ds(pl.multiple_of(SHARD - core * SHARD, SHARD), SHARD)]
    for n, group in enumerate(pending):
        for copy in group:
            copy.wait()
        yield (
            jnp.dot(own, own_buf[n], preferred_element_type=F32)
            + jnp.dot(sib, sib_buf[n], preferred_element_type=F32)
        ).astype(BF)


def finish_first(where, mine, recv, q, fresh, wo, wos, *refs):
    outs = refs[:CHIPS]
    own_buf, sib_buf, flat, att, sems = refs[CHIPS:]
    pending = out_copies(where, range(CHIPS), wo, wos, own_buf, sib_buf, sems)
    attended(mine, recv, q, [fresh], flat, att)
    for out, block in zip(outs, out_blocks(where, att, pending, own_buf, sib_buf)):
        out[...] = block


def finish_other(where, slots, mine, recv, late, late_sib, q, f1, f2, came, came_sib, wo, wos, *refs):
    half = CHIPS // 2
    before, outs = refs[:half], refs[half : 2 * half]
    att, own_buf, sib_buf, carried, flat, own_terms, sib_terms, sems = refs[2 * half :]
    pending = out_copies(where, range(half), wo, wos, own_buf, sib_buf, sems)
    carried[...] = f1[...]
    first = where[0] % 2 == 0
    keys = jnp.where(first, came[...], came_sib[...])
    values = jnp.where(first, came_sib[...], came[...])
    arrived = jnp.concatenate([keys, values], 1)
    for j in range(MOVE):
        carried[pl.ds(slots[j], 1), :] = arrived[j : j + 1]
    for kept, whole, some in ((own_terms, mine, late), (sib_terms, recv, late_sib)):
        kept[...] = whole[...]
        stats = kept[pl.ds(REQ * HEADS, HEADS), :]
        fixes = some[pl.ds(MOVE * HEADS, HEADS), :]
        for j in range(MOVE):
            at = pl.ds(pl.multiple_of(slots[j] * HEADS, HEADS), HEADS)
            kept[at, :] = some[pl.ds(j * HEADS, HEADS), :]
            stats = noted(stats, slots[j], fixes[:, j : j + 1], fixes[:, REQ + j : REQ + j + 1])
        kept[pl.ds(REQ * HEADS, HEADS), :] = stats
    attended(own_terms, sib_terms, q, [carried, f2], flat, att)
    for old, out, block in zip(before, outs, out_blocks(where, att, pending, own_buf, sib_buf)):
        out[pl.ds(0, REQ), :] = old[...]
        out[pl.ds(REQ, REQ), :] = block


def finish_same(where, att, wo, wos, *refs):
    half = CHIPS // 2
    before, outs = refs[:half], refs[half : 2 * half]
    own_buf, sib_buf, sems = refs[2 * half :]
    pending = out_copies(where, range(half, CHIPS), wo, wos, own_buf, sib_buf, sems)
    for old, out, block in zip(before, outs, out_blocks(where, att, pending, own_buf, sib_buf)):
        out[pl.ds(0, REQ), :] = old[...]
        out[pl.ds(REQ, REQ), :] = block


def shards(
    x_steps, norm_gain, w_query, w_keyval, w_out, key_cache, lengths, moved_slots, partner_mask
):
    dma = pltpu.SemaphoreType.DMA
    me = lax.axis_index("tp")
    instance = lax.axis_index("inst")
    where = jnp.reshape(me, (1,)).astype(jnp.int32)
    cache = key_cache[:, 0]

    rows = 2 * REQ
    powers = ROPE_BASE ** (-(np.arange(HD // 2, dtype=np.float32) * 2.0) / HD)
    frequency = jnp.asarray(np.concatenate([powers, powers])[None].astype(np.float32))
    slots, own_lengths, next_lengths, tables, moving, wo_send = call(
        prepare,
        [SMEM] * 4 + [VMEM] + [ANY] * 2,
        [SMEM] * 3 + [VMEM] * 2 + [ANY],
        [
            pltpu.VMEM((CHIPS, SHARD, SHARD), BF),
            pltpu.VMEM((rows, HD), F32),
            dma((CHIPS, 2)),
            dma((MOVE,)),
        ],
        [
            shape((MOVE,), jnp.int32),
            shape((REQ,), jnp.int32),
            shape((REQ,), jnp.int32),
            shape((2, rows, HD), F32),
            shape((MOVE, BLK, 2 * HD), BF),
            shape((CHIPS, SHARD, SHARD), BF),
        ],
        0,
        10 << 20,
        58,
    )(jnp.stack([me, instance]).astype(jnp.int32), moved_slots, partner_mask, lengths, frequency, cache, w_out)
    own_x = x_steps.reshape(2 * REQ, SHARD)
    own_x, slots, own_lengths, next_lengths, tables, moving, wo_send = (
        lax.optimization_barrier(
            (own_x, slots, own_lengths, next_lengths, tables, moving, wo_send)
        )
    )

    far_x = swap(own_x, "tp", 8)
    near = [own_x] + [swap(own_x, "tp", 2 * i) for i in (1, 2, 3)]
    far = [far_x] + [swap(far_x, "tp", 2 * i) for i in (1, 2, 3)]
    near_sib = swap(jnp.stack(near), "tp", 1)

    def hop(part, bit, masks):
        took = ((masks >> bit) & 1 == 1).reshape((-1,) + (1,) * (part.ndim - 1))
        return jnp.where(took, swap(part, "inst", 1 << bit), part)

    moving = hop(moving, 2, partner_mask)
    far_all, moving = lax.optimization_barrier((jnp.stack(far), moving))
    far_sib = swap(far_all, "tp", 1)
    moving = hop(moving, 1, partner_mask)

    half_chips = CHIPS // 2
    gain = norm_gain.reshape(2 * CHIPS, SHARD)
    queries, sent = call(
        project,
        [SMEM] * 2 + [VMEM] * (CHIPS + 6),
        [VMEM] * 2,
        [pltpu.VMEM((rows, OWN), F32), pltpu.VMEM((rows, HD), F32)],
        [shape((rows, OWN), BF), shape((2 * MOVE, HD), F32)],
        2 * rows * 2 * CHIPS * SHARD * OWN,
        12 << 20,
        20,
    )(
        where,
        slots,
        *near,
        near_sib,
        *far,
        far_sib,
        gain,
        w_query,
        w_keyval,
        tables,
    )
    queries_sib = swap(queries, "tp", 1)
    wos = swap(wo_send, "tp", 1)
    came = sent.astype(BF)
    masks = jnp.concatenate([partner_mask, partner_mask])
    came = hop(came, 0, masks)
    came, queries_sib, moving = lax.optimization_barrier((came, queries_sib, moving))
    moving = hop(moving, 0, partner_mask)
    came = hop(came, 1, masks)

    term_shape = shape((REQ * HEADS + HEADS, HD), F32)
    q_shape = shape((REQ * HEADS, HD), F32)
    fresh_shape = shape((REQ, 2 * HD), F32)
    kv_scratch = pltpu.VMEM((REQ, BLK, 2 * HD), BF)
    t1, q1, f1 = call(
        functools.partial(attend, 0),
        [SMEM] * 2 + [VMEM] * 2 + [ANY],
        [VMEM] * 3,
        [kv_scratch, dma((4,))],
        [term_shape, q_shape, fresh_shape],
        4 * REQ * HEADS * BLK * HD,
        6 << 20,
    )(where, own_lengths, queries, queries_sib, cache)
    t1, came = lax.optimization_barrier((t1, came))
    t1_sib = swap(t1, "tp", 1)
    came = hop(came, 2, masks)
    t2, q2, f2 = call(
        functools.partial(attend, 1),
        [SMEM] * 2 + [VMEM] * 2 + [ANY],
        [VMEM] * 3,
        [kv_scratch, dma((4,))],
        [term_shape, q_shape, fresh_shape],
        4 * REQ * HEADS * BLK * HD,
        6 << 20,
    )(where, next_lengths, queries, queries_sib, cache)
    t2, came = lax.optimization_barrier((t2, came))
    t2_sib = swap(t2, "tp", 1)
    came_sib = swap(came, "tp", 1)

    def weights(count):
        return [pltpu.VMEM((count, SHARD, SHARD), BF)] * 2

    flat = pltpu.VMEM((REQ * HEADS, HD), F32)
    block = shape((REQ, SHARD), BF)
    both = shape((rows, SHARD), BF)
    firsts = call(
        finish_first,
        [SMEM] + [VMEM] * 4 + [ANY] * 2,
        [VMEM] * CHIPS,
        weights(CHIPS) + [flat, pltpu.VMEM((REQ, QW), BF), dma((CHIPS, 2))],
        [block] * CHIPS,
        2 * REQ * QW * CHIPS * SHARD,
        10 << 20,
    )(where, t1, t1_sib, q1, f1, w_out, wos)
    first_half, moving = lax.optimization_barrier((firsts[:half_chips], moving))
    t3 = call(
        attend_arrived,
        [SMEM] * 3 + [VMEM] * 2,
        VMEM,
        [],
        shape((MOVE * HEADS + HEADS, HD), F32),
        4 * MOVE * HEADS * BLK * HD,
        1 << 20,
    )(where, next_lengths, slots, q2, moving)
    t3_sib = swap(t3, "tp", 1)
    *others, att = call(
        finish_other,
        [SMEM] * 2 + [VMEM] * 9 + [ANY] * 2 + [VMEM] * half_chips,
        [VMEM] * (half_chips + 1),
        weights(half_chips)
        + [pltpu.VMEM((REQ, 2 * HD), F32), flat]
        + [pltpu.VMEM(term_shape.shape, F32)] * 2
        + [dma((half_chips, 2))],
        [both] * half_chips + [shape((REQ, QW), BF)],
        REQ * QW * CHIPS * SHARD,
        6 << 20,
    )(
        where, slots, t2, t2_sib, t3, t3_sib, q2, f1, f2, came.astype(F32), came_sib.astype(F32), w_out, wos,
        *first_half,
    )
    sames = call(
        finish_same,
        [SMEM] + [VMEM] + [ANY] * 2 + [VMEM] * half_chips,
        [VMEM] * half_chips,
        weights(half_chips) + [dma((half_chips, 2))],
        [both] * half_chips,
        REQ * QW * CHIPS * SHARD,
        5 << 20,
    )(where, att, w_out, wos, *firsts[half_chips:])
    parts = list(others) + list(sames)

    def added(values):
        return functools.reduce(jnp.add, [value.astype(F32) for value in values])

    other = added([parts[0]] + [swap(parts[i], "tp", 2 * i) for i in (1, 2, 3)]).astype(BF)
    crossed = swap(other, "tp", 8)
    same = added([parts[4]] + [swap(parts[4 + i], "tp", 2 * i) for i in (1, 2, 3)])
    out = (same + crossed.astype(F32)).astype(BF)
    return out.reshape(2, REQ, SHARD), moving[:, None]


def solution(mesh):
    placed = (
        P(None, "inst", "tp"),
        P(),
        P(None, "tp"),
        P(None, "tp"),
        P("tp", None),
        P("inst", "tp", None, None),
        P(),
        P(),
        P(),
    )
    return jax.shard_map(
        shards,
        mesh=mesh,
        in_specs=placed,
        out_specs=(P(None, "inst", "tp"), P("inst", "tp", None, None)),
        check_vma=False,
    )
```

```python
import functools
import math

import jax
import jax.numpy as jnp
import numpy as np
from jax import lax
from jax.experimental import pallas as pl
from jax.experimental.pallas import tpu as pltpu
from jax.sharding import PartitionSpec as P

BF = jnp.bfloat16
F32 = jnp.float32
EPS = 1e-05
ROPE_BASE = 500000.0
FLOOR = -1e30
HD = 128
BLK = 128
REQ = 64
HEADS = 8
SHARD = 512
CHIPS = 8
MOVE = 8
QW = HEADS * HD
OWN = SHARD + HD
ANY = pl.BlockSpec(memory_space=pl.ANY)
VMEM = pl.BlockSpec(memory_space=pltpu.VMEM)
SMEM = pl.BlockSpec(memory_space=pltpu.SMEM)
MIB = 1024 * 1024


def call(body, ins, outs, scratch, out_shapes, flops, moved, limit=48):
    return pl.pallas_call(
        body,
        out_shape=out_shapes,
        in_specs=ins,
        out_specs=outs,
        scratch_shapes=scratch,
        compiler_params=pltpu.CompilerParams(vmem_limit_bytes=limit * MIB),
        cost_estimate=pl.CostEstimate(flops=flops, bytes_accessed=moved, transcendentals=0),
    )


def shape(dims, kind):
    return jax.ShapeDtypeStruct(dims, kind)


def swap(value, axis, mask):
    count = lax.axis_size(axis)
    return lax.ppermute(value, axis, [(i, i ^ mask) for i in range(count)])


def prepare(
    where, moved, masks, lengths, frequency, cache, wo,
    slots, own_lens, next_lens, tables, rows, wo_out, held, angle, sems, row_sems,
):
    other = 1 - where[0] % 2
    instance = where[1]
    row_copies = [
        pltpu.make_async_copy(cache.at[moved[instance, j]], rows.at[j], row_sems.at[j])
        for j in range(MOVE)
    ]
    reads = []
    writes = []
    for b in range(CHIPS):
        cols = pl.ds(pl.multiple_of((2 * b + other) * SHARD, SHARD), SHARD)
        reads.append(pltpu.make_async_copy(wo.at[:, cols], held.at[b], sems.at[b, 0]))
        writes.append(pltpu.make_async_copy(held.at[b], wo_out.at[b], sems.at[b, 1]))
    for copy in reads + row_copies:
        copy.start()
    for r in range(REQ):
        length = lengths[instance * REQ + r]
        own_lens[r] = length
        next_lens[r] = length
        angle[pl.ds(r, 1), :] = jnp.full((1, HD), length.astype(F32))
        angle[pl.ds(REQ + r, 1), :] = jnp.full((1, HD), (length + 1).astype(F32))
    for j in range(MOVE):
        slot = moved[instance, j]
        partner = instance ^ masks[j]
        length = lengths[partner * REQ + moved[partner, j]]
        slots[j] = slot
        next_lens[slot] = length
        angle[pl.ds(REQ + slot, 1), :] = jnp.full((1, HD), (length + 1).astype(F32))
    turn = angle[...] * frequency[...]
    low = lax.broadcasted_iota(jnp.int32, turn.shape, 1) < HD // 2
    wave = jnp.sin(turn)
    tables[0] = jnp.cos(turn)
    tables[1] = jnp.where(low, -wave, wave)
    for read, write in zip(reads, writes):
        read.wait()
        write.start()
    for copy in row_copies + writes:
        copy.wait()


def project(where, slots, *refs):
    near, (near_sib,) = refs[: CHIPS // 2], refs[CHIPS // 2 : CHIPS // 2 + 1]
    far, (far_sib,) = refs[CHIPS // 2 + 1 : CHIPS + 1], refs[CHIPS + 1 : CHIPS + 2]
    gain, wq, wkv, tables_in, out, sent, acc, wide, tables, sem = refs[CHIPS + 2 :]
    turns = pltpu.make_async_copy(tables_in, tables, sem)
    turns.start()
    me = where[0]
    half = CHIPS // 2
    squares = None
    for i in range(2 * CHIPS):
        src = me ^ (2 * (i % half) + (0, 1, 8, 9)[i // half])
        rows = pl.ds(pl.multiple_of(src * SHARD, SHARD), SHARD)
        ref = (near[i % half], near_sib, far[i % half], far_sib)[i // half]
        x = (ref[i % half] if i // half % 2 else ref[...]).astype(F32)
        scaled = (x * gain[pl.ds(src, 1), :]).astype(BF)
        sq = x * x
        part = sq[:, :HD] + sq[:, HD : 2 * HD] + sq[:, 2 * HD : 3 * HD] + sq[:, 3 * HD :]
        squares = part if squares is None else squares + part
        for at, weight in ((pl.ds(0, SHARD), wq), (pl.ds(SHARD, HD), wkv)):
            term = jnp.dot(scaled, weight[rows, :], preferred_element_type=F32)
            if i == 0:
                acc[:, at] = term
            else:
                acc[:, at] += term
    turns.wait()
    mean = jnp.sum(squares, -1, keepdims=True) * (1.0 / (2 * CHIPS * SHARD))
    scale = lax.rsqrt(mean + EPS)
    cos = tables[0]
    sin = tables[1]

    def turned(vec):
        return vec * cos + pltpu.roll(vec, HD // 2, 1) * sin

    for h in range(SHARD // HD):
        at = pl.ds(h * HD, HD)
        out[:, at] = turned(acc[:, at] * scale).astype(BF)
    raw = acc[:, pl.ds(SHARD, HD)] * scale
    kept = jnp.where(me % 2 == 0, turned(raw), raw).astype(BF)
    out[:, pl.ds(SHARD, HD)] = kept
    wide[...] = kept.astype(F32)
    sent[...] = jnp.zeros_like(sent)
    for j in range(MOVE):
        sent[pl.ds(j, 1), :] = wide[pl.ds(slots[j], 1), :]


def block_terms(queries, blocks, lens):
    scores = []
    for p, block in enumerate(blocks):
        both = jnp.concatenate(queries[2 * p : 2 * p + 2], 0).astype(BF)
        pair = lax.dot_general(
            both, block[:, :HD], (((1,), (1,)), ((), ())), preferred_element_type=F32
        )
        scores += [pair[:HEADS, :BLK], pair[HEADS:, BLK:]]
    lane = lax.broadcasted_iota(jnp.int32, (HEADS, BLK), 1)
    visible = jnp.concatenate([(lane < length).astype(F32) for length in lens], 0) > 0.0
    scores = jnp.where(visible, jnp.concatenate(scores, 0) * (1.0 / math.sqrt(HD)), FLOOR)
    top = jnp.max(scores, -1, keepdims=True)
    weights = jnp.where(visible, jnp.exp(scores - top), 0.0).astype(BF).astype(F32)
    total = jnp.sum(weights, -1, keepdims=True)
    zero = jnp.zeros((HEADS, BLK), F32)
    mixes = []
    for p, block in enumerate(blocks):
        at = 2 * p * HEADS
        one, two = weights[at : at + HEADS], weights[at + HEADS : at + 2 * HEADS]
        both = jnp.concatenate(
            [jnp.concatenate([one, zero], 1), jnp.concatenate([zero, two], 1)], 0
        ).astype(BF)
        mixes.append(jnp.dot(both, block[:, HD:], preferred_element_type=F32))
    return top, total, mixes


def noted(stats, slot, top, total):
    lane = lax.broadcasted_iota(jnp.int32, (HEADS, HD), 1)
    stats = jnp.where(lane == slot, top, stats)
    return jnp.where(lane == slot + REQ, total, stats)


def attend(step, where, lens, mine, recv, cache, terms, q_out, fresh_out, kv, sems):
    core = where[0] % 2
    base = core * BLK
    chunks = 4
    per = REQ // chunks
    copies = []
    for i in range(chunks):
        copies.append(
            pltpu.make_async_copy(cache.at[pl.ds(i * per, per)], kv.at[pl.ds(i * per, per)], sems.at[i])
        )
    for copy in copies:
        copy.start()
    rows = pl.ds(step * REQ, REQ)
    first = core == 0
    own = HEADS // 2

    def either(low_core, col):
        one = mine[rows, pl.ds(col, HD)].astype(F32)
        two = recv[rows, pl.ds(col, HD)].astype(F32)
        return jnp.where(first, one, two) if low_core else jnp.where(first, two, one)

    for h in range(HEADS):
        q_out[pl.ds(h, REQ, stride=HEADS), :] = either(h < own, (h % own) * HD)
    fresh_out[:, pl.ds(0, HD)] = either(True, SHARD)
    fresh_out[:, pl.ds(HD, HD)] = either(False, SHARD)

    stats = jnp.zeros((HEADS, HD), F32)
    for i in range(chunks):
        copies[i].wait()
        mine_r = range(i * per, (i + 1) * per)
        top, total, mixes = block_terms(
            [q_out[pl.ds(r * HEADS, HEADS), :] for r in mine_r],
            [kv[pl.ds(r, 2)].reshape(2 * BLK, 2 * HD) for r in mine_r[::2]],
            [jnp.clip(lens[r] - base, 0, BLK) for r in mine_r],
        )
        for j, r in enumerate(mine_r):
            at = slice(j * HEADS, (j + 1) * HEADS)
            stats = noted(stats, r, top[at], total[at])
            if j % 2 == 0:
                terms[pl.ds(r * HEADS, 2 * HEADS), :] = mixes[j // 2]
    terms[pl.ds(REQ * HEADS, HEADS), :] = stats


def attend_arrived(where, lens, slots, q, arrived, terms):
    base = where[0] % 2 * BLK
    top, total, mixes = block_terms(
        [q[pl.ds(pl.multiple_of(slots[j] * HEADS, HEADS), HEADS), :] for j in range(MOVE)],
        [arrived[pl.ds(j, 2)].reshape(2 * BLK, 2 * HD) for j in range(0, MOVE, 2)],
        [jnp.clip(lens[slots[j]] - base, 0, BLK) for j in range(MOVE)],
    )
    stats = jnp.zeros((HEADS, HD), F32)
    for j in range(MOVE):
        at = slice(j * HEADS, (j + 1) * HEADS)
        stats = noted(stats, j, top[at], total[at])
        if j % 2 == 0:
            terms[pl.ds(j * HEADS, 2 * HEADS), :] = mixes[j // 2]
    terms[pl.ds(MOVE * HEADS, HEADS), :] = stats


def attended(mine, recv, q, fresh, flat, att):
    lane = lax.broadcasted_iota(jnp.int32, (HEADS, REQ), 1)
    stats_m = mine[pl.ds(REQ * HEADS, HEADS), :]
    stats_r = recv[pl.ds(REQ * HEADS, HEADS), :]
    tops = [stats_m[:, :REQ], stats_r[:, :REQ]]
    sums = [stats_m[:, REQ:], stats_r[:, REQ:]]
    for row in fresh:
        keys = row[:, pl.ds(0, HD)].astype(BF)
        scores = lax.dot_general(
            q[...].astype(BF), keys, (((1,), (1,)), ((), ())), preferred_element_type=F32
        )
        taken = [
            jnp.where(lane == r, scores[r * HEADS : (r + 1) * HEADS], 0.0) for r in range(REQ)
        ]
        while len(taken) > 1:
            taken = [taken[i] + taken[i + 1] for i in range(0, len(taken), 2)]
        tops.append(taken[0] * (1.0 / math.sqrt(HD)))
        sums.append(1.0)
    overall = functools.reduce(jnp.maximum, tops)
    factors = [jnp.exp(top - overall) for top in tops]
    below = functools.reduce(jnp.add, [f * s for f, s in zip(factors, sums)])
    factors = [f / below for f in factors]
    for r in range(REQ):
        at = pl.ds(r * HEADS, HEADS)
        mixes = [mine[at, :], recv[at, :]] + [row[pl.ds(r, 1), pl.ds(HD, HD)] for row in fresh]
        flat[at, :] = functools.reduce(
            jnp.add, [f[:, r : r + 1] * mix for f, mix in zip(factors, mixes)]
        )
    for h in range(HEADS):
        att[:, pl.ds(h * HD, HD)] = flat[
            pl.ds(h, REQ, stride=HEADS), :
        ].astype(BF)


def out_copies(where, blocks, wo, wos, own_buf, sib_buf, sems):
    me = where[0]
    pending = []
    for n, i in enumerate(blocks):
        dst = me ^ (8 + 2 * i if i < 4 else 2 * (i - 4))
        cols = pl.ds(pl.multiple_of(dst * SHARD, SHARD), SHARD)
        group = [
            pltpu.make_async_copy(wo.at[:, cols], own_buf.at[n], sems.at[n, 0]),
            pltpu.make_async_copy(wos.at[dst // 2], sib_buf.at[n], sems.at[n, 1]),
        ]
        for copy in group:
            copy.start()
        pending.append(group)
    return pending


def out_blocks(where, att, pending, own_buf, sib_buf):
    core = where[0] % 2
    own = att[:, pl.ds(pl.multiple_of(core * SHARD, SHARD), SHARD)]
    sib = att[:, pl.ds(pl.multiple_of(SHARD - core * SHARD, SHARD), SHARD)]
    for n, group in enumerate(pending):
        for copy in group:
            copy.wait()
        yield (
            jnp.dot(own, own_buf[n], preferred_element_type=F32)
            + jnp.dot(sib, sib_buf[n], preferred_element_type=F32)
        ).astype(BF)


def combine_first(mine, recv, q, fresh, att, flat):
    attended(mine, recv, q, [fresh], flat, att)


def finish_other(where, slots, mine, recv, late, late_sib, q, f1, f2, came, came_sib, wo, wos, first, *refs):
    half = CHIPS // 2
    outs = refs[:half]
    att, own_buf, sib_buf, carried, flat, own_terms, sib_terms, sems = refs[half:]
    pending = out_copies(where, range(half), wo, wos, own_buf, sib_buf, sems)
    carried[...] = f1[...]
    low = where[0] % 2 == 0
    keys = jnp.where(low, came[...], came_sib[...])
    values = jnp.where(low, came_sib[...], came[...])
    arrived = jnp.concatenate([keys, values], 1)
    for j in range(MOVE):
        carried[pl.ds(slots[j], 1), :] = arrived[j : j + 1]
    for kept, whole, some in ((own_terms, mine, late), (sib_terms, recv, late_sib)):
        kept[...] = whole[...]
        stats = kept[pl.ds(REQ * HEADS, HEADS), :]
        fixes = some[pl.ds(MOVE * HEADS, HEADS), :]
        for j in range(MOVE):
            at = pl.ds(pl.multiple_of(slots[j] * HEADS, HEADS), HEADS)
            kept[at, :] = some[pl.ds(j * HEADS, HEADS), :]
            stats = noted(stats, slots[j], fixes[:, j : j + 1], fixes[:, REQ + j : REQ + j + 1])
        kept[pl.ds(REQ * HEADS, HEADS), :] = stats
    att[pl.ds(0, REQ), :] = first[...]
    attended(own_terms, sib_terms, q, [carried, f2], flat, att.at[pl.ds(REQ, REQ), :])
    for out, block in zip(outs, out_blocks(where, att, pending, own_buf, sib_buf)):
        out[...] = block


def finish_same(where, att, wo, wos, *refs):
    half = CHIPS // 2
    outs = refs[:half]
    own_buf, sib_buf, sems = refs[half:]
    pending = out_copies(where, range(half, CHIPS), wo, wos, own_buf, sib_buf, sems)
    for out, block in zip(outs, out_blocks(where, att, pending, own_buf, sib_buf)):
        out[...] = block


def shards(
    x_steps, norm_gain, w_query, w_keyval, w_out, key_cache, lengths, moved_slots, partner_mask
):
    dma = pltpu.SemaphoreType.DMA
    me = lax.axis_index("tp")
    instance = lax.axis_index("inst")
    where = jnp.reshape(me, (1,)).astype(jnp.int32)
    cache = key_cache[:, 0]

    rows = 2 * REQ
    powers = ROPE_BASE ** (-(np.arange(HD // 2, dtype=np.float32) * 2.0) / HD)
    frequency = jnp.asarray(np.concatenate([powers, powers])[None].astype(np.float32))
    slots, own_lengths, next_lengths, tables, moving, wo_send = call(
        prepare,
        [SMEM] * 4 + [VMEM] + [ANY] * 2,
        [SMEM] * 3 + [VMEM] * 2 + [ANY],
        [
            pltpu.VMEM((CHIPS, SHARD, SHARD), BF),
            pltpu.VMEM((rows, HD), F32),
            dma((CHIPS, 2)),
            dma((MOVE,)),
        ],
        [
            shape((MOVE,), jnp.int32),
            shape((REQ,), jnp.int32),
            shape((REQ,), jnp.int32),
            shape((2, rows, HD), F32),
            shape((MOVE, BLK, 2 * HD), BF),
            shape((CHIPS, SHARD, SHARD), BF),
        ],
        0,
        10 << 20,
        58,
    )(jnp.stack([me, instance]).astype(jnp.int32), moved_slots, partner_mask, lengths, frequency, cache, w_out)
    own_x = x_steps.reshape(2 * REQ, SHARD)
    own_x, slots, own_lengths, next_lengths, tables, moving, wo_send = (
        lax.optimization_barrier(
            (own_x, slots, own_lengths, next_lengths, tables, moving, wo_send)
        )
    )

    far_x = swap(own_x, "tp", 8)
    near = [own_x] + [swap(own_x, "tp", 2 * i) for i in (1, 2, 3)]
    far = [far_x] + [swap(far_x, "tp", 2 * i) for i in (1, 2, 3)]
    near_sib = swap(jnp.stack(near), "tp", 1)

    def hop(part, bit, masks):
        took = ((masks >> bit) & 1 == 1).reshape((-1,) + (1,) * (part.ndim - 1))
        return jnp.where(took, swap(part, "inst", 1 << bit), part)

    moving = hop(moving, 2, partner_mask)
    far_sib = swap(jnp.stack(far), "tp", 1)
    moving = hop(moving, 1, partner_mask)

    half_chips = CHIPS // 2
    gain = norm_gain.reshape(2 * CHIPS, SHARD)
    queries, sent = call(
        project,
        [SMEM] * 2 + [VMEM] * (CHIPS + 5) + [ANY],
        [VMEM] * 2,
        [
            pltpu.VMEM((rows, OWN), F32),
            pltpu.VMEM((rows, HD), F32),
            pltpu.VMEM((2, rows, HD), F32),
            dma,
        ],
        [shape((rows, OWN), BF), shape((2 * MOVE, HD), F32)],
        2 * rows * 2 * CHIPS * SHARD * OWN,
        12 << 20,
        20,
    )(
        where,
        slots,
        *near,
        near_sib,
        *far,
        far_sib,
        gain,
        w_query,
        w_keyval,
        tables,
    )
    queries_sib = swap(queries, "tp", 1)
    wos = swap(wo_send, "tp", 1)
    came = sent.astype(BF)
    masks = jnp.concatenate([partner_mask, partner_mask])
    came = hop(came, 0, masks)
    came, queries_sib, moving = lax.optimization_barrier((came, queries_sib, moving))
    moving = hop(moving, 0, partner_mask)
    came = hop(came, 1, masks)

    term_shape = shape((REQ * HEADS + HEADS, HD), F32)
    q_shape = shape((REQ * HEADS, HD), F32)
    fresh_shape = shape((REQ, 2 * HD), F32)
    kv_scratch = pltpu.VMEM((REQ, BLK, 2 * HD), BF)
    t1, q1, f1 = call(
        functools.partial(attend, 0),
        [SMEM] * 2 + [VMEM] * 2 + [ANY],
        [VMEM] * 3,
        [kv_scratch, dma((4,))],
        [term_shape, q_shape, fresh_shape],
        4 * REQ * HEADS * BLK * HD,
        6 << 20,
    )(where, own_lengths, queries, queries_sib, cache)
    t1, came = lax.optimization_barrier((t1, came))
    t1_sib = swap(t1, "tp", 1)
    t2, q2, f2 = call(
        functools.partial(attend, 1),
        [SMEM] * 2 + [VMEM] * 2 + [ANY],
        [VMEM] * 3,
        [kv_scratch, dma((4,))],
        [term_shape, q_shape, fresh_shape],
        4 * REQ * HEADS * BLK * HD,
        6 << 20,
    )(where, next_lengths, queries, queries_sib, cache)
    t2, came = lax.optimization_barrier((t2, came))
    t2_sib = swap(t2, "tp", 1)
    came = hop(came, 2, masks)
    came_sib = swap(came, "tp", 1)

    def weights(count):
        return [pltpu.VMEM((count, SHARD, SHARD), BF)] * 2

    flat = pltpu.VMEM((REQ * HEADS, HD), F32)
    both = shape((rows, SHARD), BF)
    att_first = call(
        combine_first,
        [VMEM] * 4,
        VMEM,
        [flat],
        shape((REQ, QW), BF),
        1 << 20,
        1 << 20,
    )(t1, t1_sib, q1, f1)
    t3 = call(
        attend_arrived,
        [SMEM] * 3 + [VMEM] * 2,
        VMEM,
        [],
        shape((MOVE * HEADS + HEADS, HD), F32),
        4 * MOVE * HEADS * BLK * HD,
        1 << 20,
    )(where, next_lengths, slots, q2, moving)
    t3_sib = swap(t3, "tp", 1)
    *others, att = call(
        finish_other,
        [SMEM] * 2 + [VMEM] * 9 + [ANY] * 2 + [VMEM],
        [VMEM] * (half_chips + 1),
        weights(half_chips)
        + [pltpu.VMEM((REQ, 2 * HD), F32), flat]
        + [pltpu.VMEM(term_shape.shape, F32)] * 2
        + [dma((half_chips, 2))],
        [both] * half_chips + [shape((rows, QW), BF)],
        2 * REQ * QW * CHIPS * SHARD,
        6 << 20,
    )(
        where, slots, t2, t2_sib, t3, t3_sib, q2, f1, f2, came.astype(F32), came_sib.astype(F32), w_out, wos,
        att_first,
    )
    sames = call(
        finish_same,
        [SMEM] + [VMEM] + [ANY] * 2,
        [VMEM] * half_chips,
        weights(half_chips) + [dma((half_chips, 2))],
        [both] * half_chips,
        REQ * QW * CHIPS * SHARD,
        5 << 20,
    )(where, att, w_out, wos)
    parts = list(others) + list(sames)

    def added(values):
        return functools.reduce(jnp.add, [value.astype(F32) for value in values])

    other = added([parts[0]] + [swap(parts[i], "tp", 2 * i) for i in (1, 2, 3)]).astype(BF)
    crossed = swap(other, "tp", 8)
    same = added([parts[4]] + [swap(parts[4 + i], "tp", 2 * i) for i in (1, 2, 3)])
    out = (same + crossed.astype(F32)).astype(BF)
    return out.reshape(2, REQ, SHARD), moving[:, None]


def solution(mesh):
    placed = (
        P(None, "inst", "tp"),
        P(),
        P(None, "tp"),
        P(None, "tp"),
        P("tp", None),
        P("inst", "tp", None, None),
        P(),
        P(),
        P(),
    )
    return jax.shard_map(
        shards,
        mesh=mesh,
        in_specs=placed,
        out_specs=(P(None, "inst", "tp"), P("inst", "tp", None, None)),
        check_vma=False,
    )
```
